512 devices in a mesh: dp: 32 (over z, x_lo), seq: 16 (over x_hi, y, core).
Axes of the slice: x: 4 (x_hi: 2, x_lo: 2; x = x_hi * 2 + x_lo), y: 4, z: 16, core: 2. Of those that a mesh axis runs over, the one named last changes fastest.
Arguments:
- image_projected: bfloat16 [32, 2048, 3, 2048], P('dp', 'seq'), may hold values from -8 to 8
- text_projected: bfloat16 [32, 512, 3, 2048], P('dp', 'seq'), may hold values from -8 to 8
- image_stream: bfloat16 [32, 2048, 3072], P('dp', 'seq'), may hold values from -3 to 3
- latents: float32 [32, 2048, 64], P('dp', 'seq'), may hold values from -6 to 6
- timesteps: int32 [32], P('dp'), may hold values from 0 to 9
- prompts: int32 [32], P('dp'), may hold values from 0 to 63
- noise_seeds: int32 [32], P('dp'), may hold values from 0 to 99999
- time_gate: bfloat16 [10, 3072], replicated, may hold values from -3 to 3
- prompt_gate: bfloat16 [64, 3072], replicated, may hold values from -3 to 3
- final_weight: bfloat16 [3072, 64], replicated, may hold values from -0.109375 to 0.109375
- saved_attention: bfloat16 [8192, 2048], P('dp'), may hold values from -6 to 6
- output_cotangent: bfloat16 [8192, 3072], P('dp', 'seq'), may hold values from -0.15625 to 0.15625
- master_weight: float32 [2048, 3072], P('dp', 'seq'), may hold values from -0.125 to 0.125
- first_moment: float32 [2048, 3072], P('dp', 'seq'), may hold values from -1.5 to 1.5
- second_moment: float32 [2048, 3072], P('dp', 'seq'), may hold values from 0.001 to 1
- average_weight: float32 [2048, 3072], P('dp', 'seq'), may hold values from -0.125 to 0.125
Outputs:
- velocity: float32 [32, 2048, 64], P('dp', 'seq')
- new_latents: float32 [32, 2048, 64], P('dp', 'seq')
- new_master: float32 [2048, 3072], P('dp', 'seq')
- new_first: float32 [2048, 3072], P('dp', 'seq')
- new_second: float32 [2048, 3072], P('dp', 'seq')
- new_average: float32 [2048, 3072], P('dp', 'seq')
The draws below stay inside these ranges and needn't reach their ends.
All inputs are finite; a program needn't handle non-finite values.
Results may differ from the reference program's by a relative error of at most 0.025.
Values may be sent and summed in bfloat16 or wider, within the bound.
No kernel may reach another device: no remote copies, remote signals or barrier semaphores. Data moves between devices by JAX's collectives and lax.ppermute only.
A program may use at most 64 MiB of HBM per device.

```python
import math
import jax
import jax.numpy as jnp
from jax import lax

D = 3072
HEAD_DIM = 128
HEADS = 16
CH = 64
STEPS = 10
PROMPTS = 64
STEP_COUNT = 100
ATT = 2048
IMG = 2048
TXT = 512
SAMPLES = 32
TRAIN_TOKENS = 8192


def draw_image_projected(key, part):
    key = jax.random.fold_in(key, 11)
    shape = (SAMPLES, IMG, 3, ATT)
    base = jnp.clip(2.0 * jax.random.normal(key, shape, jnp.float32), -8.0, 8.0)
    return base.astype(jnp.bfloat16)


def place_ends(drawn, own_key, smallest, high):
    shape = drawn.shape
    place = [jax.random.randint(jax.random.fold_in(own_key, axis), (), 0, shape[axis]) for axis in range(len(shape))]
    drawn = drawn.at[tuple(place)].set(smallest)
    longest = shape.index(max(shape))
    place[longest] = (place[longest] + 1) % shape[longest]
    return drawn.at[tuple(place)].set(high)


def spiked(values, key, source, target, parts, factor):
    def block_of(axis_at):
        return (jnp.arange(values.shape[axis_at]) // (values.shape[axis_at] // parts)).reshape((-1,) + (1,) * (values.ndim - 1 - axis_at))

    near = jax.random.permutation(key, parts)[block_of(target)]
    far = (block_of(target) + parts // 2) % parts
    return jnp.where((block_of(source) == near) | (block_of(source) == far), factor * values, values)


def level_of(key, shape, pieces, smallest, top_value):
    gain = 1.0
    for dim, parts in pieces:
        steps = jax.random.uniform(jax.random.fold_in(jax.random.fold_in(key, 6), dim), (parts,), jnp.float32, smallest / len(pieces), top_value / len(pieces))
        gain = gain * jnp.repeat(jnp.exp(steps), shape[dim] // parts).reshape((-1,) + (1,) * (len(shape) - 1 - dim))
    return gain


def bell_draw(rng, shape, spread, reach, split=(), kind=jnp.bfloat16):
    result = spread * jax.random.normal(rng, shape, jnp.float32)
    if split:
        result = result * level_of(rng, shape, split, -0.22, 0.18)
    return jnp.clip(result, -reach, reach).astype(kind)


def heavy_noise(stream_key, shape, spread, limit, pieces, heavy, kind=jnp.bfloat16):
    drawn = spread * jax.random.normal(stream_key, shape, jnp.float32)
    if pieces:
        drawn = drawn * level_of(stream_key, shape, pieces, -0.22, 0.18)
    return jnp.clip(spiked(drawn, jax.random.fold_in(stream_key, 3), *heavy), -limit, limit).astype(kind)


def setup_inputs(seed: int = 0) -> dict:
    key_list = jax.random.split(jax.random.key(seed), 17)
    return {
        "image_projected": draw_image_projected(jax.random.fold_in(key_list[16], 71), 0),
        "text_projected": bell_draw(key_list[1], (SAMPLES, TXT, 3, ATT), 2.0, 8.0, ((0, 32), (1, 16))),
        "image_stream": bell_draw(key_list[2], (SAMPLES, IMG, D), 0.5, 3.0, ((0, 32), (1, 16))),
        "latents": bell_draw(key_list[3], (SAMPLES, IMG, CH), 1.0, 6.0, ((0, 32), (1, 16)), jnp.float32),
        "timesteps": place_ends(jax.random.randint(key_list[4], (SAMPLES,), 0, STEPS), jax.random.fold_in(key_list[4], 1), 0, STEPS - 1).astype(jnp.int32),
        "prompts": place_ends(jax.random.randint(key_list[5], (SAMPLES,), 0, PROMPTS), jax.random.fold_in(key_list[5], 1), 0, PROMPTS - 1).astype(jnp.int32),
        "noise_seeds": place_ends(jax.random.randint(key_list[6], (SAMPLES,), 0, 100000), jax.random.fold_in(key_list[6], 1), 0, 99999).astype(jnp.int32),
        "time_gate": bell_draw(key_list[7], (STEPS, D), 0.5, 3.0),
        "prompt_gate": bell_draw(key_list[8], (PROMPTS, D), 0.5, 3.0),
        "final_weight": bell_draw(key_list[9], (D, CH), D ** -0.5, 0.109375),
        "saved_attention": heavy_noise(key_list[10], (TRAIN_TOKENS, ATT), 1.0, 6.0, ((0, 32),), (0, 1, 32, 2.75)),
        "output_cotangent": bell_draw(key_list[11], (TRAIN_TOKENS, D), (TRAIN_TOKENS ** -0.5), 0.15625, ((0, 32), (1, 16))),
        "master_weight": bell_draw(key_list[12], (ATT, D), ATT ** -0.5, 0.125, ((0, 32), (1, 16)), jnp.float32),
        "first_moment": bell_draw(key_list[13], (ATT, D), 0.1, 1.5, ((0, 32), (1, 16)), jnp.float32),
        "second_moment": jnp.clip(jnp.exp(math.log(1.0) - 6.9077552 * jax.random.uniform(key_list[14], (ATT, D), jnp.float32) ** level_of(key_list[14], (ATT, D), ((0, 32), (1, 16)), -0.2, 0.2)), 0.001, 1.0),
        "average_weight": bell_draw(key_list[15], (ATT, D), ATT ** -0.5, 0.125, ((0, 32), (1, 16)), jnp.float32),
    }


beta_first = 0.9
beta_second = 0.999
adam_epsilon = 1e-08
learn_rate = 0.0001
average_decay = 0.99
noise_level = 0.7
norm_epsilon = 1e-06

def hashed_noise(seed_value, token_index, channel_index):
    mixed_bits = seed_value * 73856093 + token_index * 19349663 + channel_index * 83492791
    mixed_bits = mixed_bits ^ jnp.right_shift(mixed_bits, 13)
    mixed_bits = mixed_bits * 1274126177
    mixed_bits = mixed_bits ^ jnp.right_shift(mixed_bits, 16)
    low_bits = mixed_bits & 65535
    return ((low_bits.astype(jnp.float32) + 0.5) / 32768.0 - 1.0) * math.sqrt(3.0)

def reference(image_projected, text_projected, image_stream, latents, timesteps, prompts, noise_seeds, time_gate, prompt_gate, final_weight, saved_attention, output_cotangent, master_weight, first_moment, second_moment, average_weight):
    gradient = jnp.dot(saved_attention.T, output_cotangent, preferred_element_type=jnp.float32)
    new_first = beta_first * first_moment + (1.0 - beta_first) * gradient
    new_second = beta_second * second_moment + (1.0 - beta_second) * gradient * gradient
    first_corr = 1.0 - beta_first ** STEP_COUNT
    second_corr = 1.0 - beta_second ** STEP_COUNT
    new_master = master_weight - learn_rate * (new_first / first_corr) / (jnp.sqrt(new_second / second_corr) + adam_epsilon)
    new_average = average_decay * average_weight + (1.0 - average_decay) * new_master
    sampler_weight = average_weight.astype(jnp.bfloat16)
    score_scale = HEAD_DIM ** (-0.5)
    token_index = jnp.arange(IMG, dtype=jnp.int32)[:, None]
    channel_index = jnp.arange(CH, dtype=jnp.int32)[None, :]

    def one_sample(packed):
        image_part, text_part, stream, latent_now, step_index, prompt_index, seed_value = packed
        queries = image_part[:, 0].reshape(IMG, HEADS, HEAD_DIM).astype(jnp.float32)
        keys = jnp.concatenate([image_part[:, 1], text_part[:, 1]], 0).reshape(IMG + TXT, HEADS, HEAD_DIM).astype(jnp.float32)
        values = jnp.concatenate([image_part[:, 2], text_part[:, 2]], 0).reshape(IMG + TXT, HEADS, HEAD_DIM).astype(jnp.float32)
        scores = jnp.einsum('qhd,khd->hqk', queries, keys) * score_scale
        peak_score = lax.optimization_barrier(jnp.max(scores, axis=-1, keepdims=True))
        expo = jnp.exp(scores - peak_score)
        denominator = lax.optimization_barrier(jnp.sum(expo, axis=-1))
        weights = expo.astype(jnp.bfloat16).astype(jnp.float32)
        mixed = jnp.einsum('hqk,khd->qhd', weights, values) / jnp.transpose(denominator)[:, :, None]
        attention = mixed.astype(jnp.bfloat16).reshape(IMG, ATT)
        branch = jnp.dot(attention, sampler_weight, preferred_element_type=jnp.float32)
        gate = time_gate[step_index].astype(jnp.float32) + prompt_gate[prompt_index].astype(jnp.float32)
        hidden = stream.astype(jnp.float32) + gate[None, :] * branch
        mean_value = lax.optimization_barrier(jnp.mean(hidden, axis=-1, keepdims=True))
        centered = hidden - mean_value
        variance = lax.optimization_barrier(jnp.mean(centered * centered, axis=-1, keepdims=True))
        normalized = (centered / jnp.sqrt(variance + norm_epsilon)).astype(jnp.bfloat16)
        velocity = jnp.dot(normalized, final_weight, preferred_element_type=jnp.float32)
        step_float = step_index.astype(jnp.float32)
        time_now = 1.0 - (step_float + 1.0) / (STEPS + 2.0)
        time_next = 1.0 - (step_float + 2.0) / (STEPS + 2.0)
        sigma = noise_level * jnp.sqrt(time_now / (1.0 - time_now))
        noise = hashed_noise(seed_value, token_index, channel_index)
        drift = velocity + sigma * sigma / (2.0 * time_now) * (latent_now + (1.0 - time_now) * velocity)
        stepped = latent_now + drift * (time_next - time_now) + sigma * jnp.sqrt(time_now - time_next) * noise
        return (velocity, stepped)
    velocity, new_latents = lax.map(one_sample, (image_projected, text_projected, image_stream, latents, timesteps, prompts, noise_seeds))
    return (velocity, new_latents, new_master, new_first, new_second, new_average)
```

```python
import functools
import math

import jax
import jax.numpy as jnp
from jax import lax
from jax.experimental import pallas as pl
from jax.experimental.pallas import tpu as pltpu
from jax.sharding import PartitionSpec as P

HEAD_DIM = 128
STEPS = 10
STEP_COUNT = 100


beta_first = 0.9
beta_second = 0.999
adam_epsilon = 1e-08
learn_rate = 0.0001
average_decay = 0.99
noise_level = 0.7
norm_epsilon = 1e-06


def hashed_noise(seed_value, token_index, channel_index):
    mixed_bits = seed_value * 73856093 + token_index * 19349663 + channel_index * 83492791
    mixed_bits = mixed_bits ^ jnp.right_shift(mixed_bits, 13)
    mixed_bits = mixed_bits * 1274126177
    mixed_bits = mixed_bits ^ jnp.right_shift(mixed_bits, 16)
    low_bits = mixed_bits & 65535
    return ((low_bits.astype(jnp.float32) + 0.5) / 32768.0 - 1.0) * math.sqrt(3.0)


AXES = ("z", "xl", "xh", "y", "c")
DP = ("z", "xl")
SEQ = ("xh", "y", "c")
MEBI = 1024 * 1024
VMEM = pl.BlockSpec(memory_space=pltpu.VMEM)
SMEM = pl.BlockSpec(memory_space=pltpu.SMEM)


def pack_kernel(image_ref, text_ref, out_ref):
    heads, _, _, width = out_ref.shape
    image_tokens = image_ref.shape[1]
    for head in range(heads):
        span = slice(head * width, (head + 1) * width)
        out_ref[head, :, :image_tokens, :] = image_ref[:, :, span]
        out_ref[head, :, image_tokens:, :] = text_ref[:, :, span]


def pack(image, text):
    tokens = image.shape[1] + text.shape[1]
    return pl.pallas_call(
        pack_kernel,
        out_shape=jax.ShapeDtypeStruct((16, 3, tokens, HEAD_DIM), jnp.bfloat16),
        in_specs=[VMEM, VMEM],
        out_specs=VMEM,
        compiler_params=pltpu.CompilerParams(vmem_limit_bytes=16 * MEBI),
        name="pack",
    )(image, text)


def attention_kernel(packed_ref, out_ref, widened_ref):
    sources, _, tokens, width = packed_ref.shape
    image_tokens = out_ref.shape[2]
    scale = width ** (-0.5) * math.log2(math.e)
    keys = packed_ref[:, 1].reshape(sources * tokens, width)
    widened_ref[:, :width] = packed_ref[:, 2].reshape(sources * tokens, width)
    widened_ref[:, width:] = jnp.ones((sources * tokens, width), jnp.bfloat16)

    def step(index, carry):
        queries = packed_ref[pl.ds(index * 2, 2), 0, :image_tokens, :]
        queries = queries.reshape(2 * image_tokens, width)
        scores = lax.dot_general(
            queries, keys, (((1,), (1,)), ((), ())), preferred_element_type=jnp.float32
        )
        peak = jnp.max(scores, axis=-1, keepdims=True)
        expo = jnp.exp2((scores - peak) * scale)
        mixed = jnp.dot(
            expo.astype(jnp.bfloat16), widened_ref[...], preferred_element_type=jnp.float32
        )
        result = (mixed[:, :width] / mixed[:, width:]).astype(jnp.bfloat16)
        row = index % 4
        half = index // 4
        for core in range(2):
            block = result[core * image_tokens : (core + 1) * image_tokens]
            for target in range(4):
                out_ref[half * 8 + target * 2 + core, row] = block
        return carry

    lax.fori_loop(0, sources // 2, step, 0, unroll=2)


def attend(packed, image_tokens):
    sources, _, tokens, width = packed.shape
    return pl.pallas_call(
        attention_kernel,
        out_shape=jax.ShapeDtypeStruct((16, 4, image_tokens, HEAD_DIM), jnp.bfloat16),
        in_specs=[VMEM],
        out_specs=VMEM,
        scratch_shapes=[pltpu.VMEM((sources * tokens, 2 * width), jnp.bfloat16)],
        compiler_params=pltpu.CompilerParams(vmem_limit_bytes=24 * MEBI),
        cost_estimate=pl.CostEstimate(
            flops=2700000000, bytes_accessed=4000000, transcendentals=5300000
        ),
        name="attend",
    )(packed)


def project_kernel(heads_ref, weight_ref, out_ref, flat_ref):
    head_count, _, width = heads_ref.shape
    for head in range(head_count):
        flat_ref[:, head * width : (head + 1) * width] = heads_ref[head]
    out_ref[...] = jnp.dot(
        flat_ref[...], weight_ref[...], preferred_element_type=jnp.float32
    ).astype(jnp.bfloat16)


def project(heads, weight):
    head_count, tokens, width = heads.shape
    return pl.pallas_call(
        project_kernel,
        out_shape=jax.ShapeDtypeStruct((tokens, weight.shape[1]), jnp.bfloat16),
        in_specs=[VMEM, VMEM],
        out_specs=VMEM,
        scratch_shapes=[pltpu.VMEM((tokens, head_count * width), jnp.bfloat16)],
        compiler_params=pltpu.CompilerParams(vmem_limit_bytes=24 * MEBI),
        cost_estimate=pl.CostEstimate(
            flops=1600000000, bytes_accessed=6000000, transcendentals=0
        ),
        name="project",
    )(heads, weight)


def finish_kernel(
    slope_ref, branch_ref, stream_ref, gate_ref, final_ref, base_ref, velocity_ref, stepped_ref, hidden_ref
):
    quarters, _, columns = branch_ref.shape
    half = columns // 2
    features = stream_ref.shape[1]
    total = 0.0
    for far in range(2):
        for quarter in range(quarters):
            start = far * quarters * half + quarter * half
            span = slice(start, start + half)
            part = branch_ref[quarter, :, far * half : (far + 1) * half].astype(jnp.float32)
            hidden = stream_ref[:, span].astype(jnp.float32) + gate_ref[:, span] * part
            hidden_ref[:, span] = hidden
            total = total + jnp.sum(hidden, axis=-1, keepdims=True)
    centered = hidden_ref[...] - total / features
    variance = jnp.sum(centered * centered, axis=-1, keepdims=True) / features
    normalized = (centered * lax.rsqrt(variance + norm_epsilon)).astype(jnp.bfloat16)
    velocity = lax.dot_general(
        final_ref[...],
        normalized,
        (((1,), (1,)), ((), ())),
        preferred_element_type=jnp.float32,
    )
    velocity_ref[...] = velocity
    stepped_ref[...] = base_ref[...] + slope_ref[0] * velocity


def finish(slope, branch, stream, gate, final, base):
    shape = jax.ShapeDtypeStruct(base.shape, jnp.float32)
    return pl.pallas_call(
        finish_kernel,
        out_shape=(shape, shape),
        in_specs=[SMEM, VMEM, VMEM, VMEM, VMEM, VMEM],
        out_specs=(VMEM, VMEM),
        scratch_shapes=[pltpu.VMEM(stream.shape, jnp.float32)],
        compiler_params=pltpu.CompilerParams(vmem_limit_bytes=16 * MEBI),
        name="finish",
    )(slope, branch, stream, gate, final, base)


def deal(bit, blocks, run, keep_ref, give_ref):
    pairs = blocks.reshape((blocks.shape[0] // (2 * run), 2, run) + blocks.shape[1:])
    even = pairs[:, 0].reshape(keep_ref.shape)
    odd = pairs[:, 1].reshape(keep_ref.shape)
    keep_ref[...] = jnp.where(bit == 0, even, odd)
    give_ref[...] = jnp.where(bit == 0, odd, even)


def partial_kernel(run, bit_ref, saved_ref, cotangent_ref, keep_ref, give_ref):
    partial = lax.dot_general(
        saved_ref[...],
        cotangent_ref[...],
        (((0,), (0,)), ((), ())),
        preferred_element_type=jnp.float32,
    ).astype(jnp.bfloat16)
    rows, columns = keep_ref.shape[1:]
    blocks = partial.reshape(partial.shape[0] // rows, rows, columns)
    deal(bit_ref[0], blocks, run, keep_ref, give_ref)


def merge_kernel(run, bit_ref, kept_ref, taken_ref, keep_ref, give_ref):
    total = kept_ref[...].astype(jnp.float32) + taken_ref[...].astype(jnp.float32)
    deal(bit_ref[0], total.astype(jnp.bfloat16), run, keep_ref, give_ref)


def split_call(kernel, run, bit, first, second, blocks, rows, columns, name):
    half = jax.ShapeDtypeStruct((blocks // 2, rows, columns), jnp.bfloat16)
    return pl.pallas_call(
        functools.partial(kernel, run),
        out_shape=(half, half),
        in_specs=[SMEM, VMEM, VMEM],
        out_specs=(VMEM, VMEM),
        compiler_params=pltpu.CompilerParams(vmem_limit_bytes=16 * MEBI),
        name=name,
    )(bit, first, second)


def axis_bit(axis, distance):
    return ((lax.axis_index(axis) // distance) % 2).astype(jnp.int32).reshape(1)


def exchange(value, axis, distance):
    size = lax.axis_size(axis)
    return lax.ppermute(value, axis, [(k, k ^ distance) for k in range(size)])


def beside(own, other, axis, dimension):
    first = lax.axis_index(axis) == 0
    return jnp.concatenate([jnp.where(first, own, other), jnp.where(first, other, own)], dimension)


def local(
    image_projected,
    text_projected,
    image_stream,
    latents,
    timesteps,
    prompts,
    noise_seeds,
    time_gate,
    prompt_gate,
    final_weight,
    saved_attention,
    output_cotangent,
    master_weight,
    first_moment,
    second_moment,
    average_weight,
):
    image_tokens = image_projected.shape[1]
    own_rows, own_columns = master_weight.shape

    packed = pack(image_projected[0].transpose(1, 0, 2), text_projected[0].transpose(1, 0, 2))

    def share(kernel, step, first, second):
        axis, distance, run = order[step]
        return split_call(
            kernel,
            run,
            axis_bit(axis, distance),
            first,
            second,
            32 >> step,
            own_rows,
            own_columns,
            kernel.__name__[:-7],
        )

    order = (("z", 1, 2), ("z", 2, 2), ("xl", 1, 1), ("z", 4, 1), ("z", 8, 1))
    keep, give = share(partial_kernel, 0, saved_attention, output_cotangent)
    taken = exchange(give, "z", 1)

    sampler_weight = lax.optimization_barrier(average_weight.astype(jnp.bfloat16))
    pieces = beside(sampler_weight, exchange(sampler_weight, "c", 1), "c", 1)
    pieces = beside(pieces, exchange(pieces, "xh", 1), "xh", 1)
    pieces = beside(pieces, exchange(pieces, "xl", 1), "xl", 0)
    pieces, taken, packed = lax.optimization_barrier((pieces, taken, packed))
    weight = lax.all_gather(pieces, "z", axis=0, tiled=True)

    arrived = lax.all_to_all(packed, SEQ, split_axis=0, concat_axis=0, tiled=True)
    for step in range(1, len(order)):
        keep, give = share(merge_kernel, step, keep, taken)
        if step == 3:
            keep, give, arrived = lax.optimization_barrier((keep, give, arrived))
        taken = exchange(give, *order[step][:2])

    heads_out = attend(arrived, image_tokens)
    heads = lax.all_to_all(heads_out, SEQ, split_axis=0, concat_axis=0, tiled=True)
    heads, keep, taken = lax.optimization_barrier((heads, keep, taken))
    heads = heads.reshape(16, 4 * image_tokens, HEAD_DIM)

    gradient = keep[0].astype(jnp.float32) + taken[0].astype(jnp.float32)
    new_first = beta_first * first_moment + (1.0 - beta_first) * gradient
    new_second = beta_second * second_moment + (1.0 - beta_second) * gradient * gradient
    first_corr = 1.0 - beta_first**STEP_COUNT
    second_corr = 1.0 - beta_second**STEP_COUNT
    new_master = master_weight - learn_rate * (new_first / first_corr) / (
        jnp.sqrt(new_second / second_corr) + adam_epsilon
    )
    new_average = average_decay * average_weight + (1.0 - average_decay) * new_master

    step_index = timesteps[0]
    prompt_index = prompts[0]
    step_table = jnp.arange(time_gate.shape[0], dtype=jnp.int32)[:, None]
    prompt_table = jnp.arange(prompt_gate.shape[0], dtype=jnp.int32)[:, None]
    gate = jnp.sum(
        jnp.where(step_table == step_index, time_gate.astype(jnp.float32), 0.0), 0, keepdims=True
    )
    gate = gate + jnp.sum(
        jnp.where(prompt_table == prompt_index, prompt_gate.astype(jnp.float32), 0.0),
        0,
        keepdims=True,
    )
    latent_now = latents[0].transpose(1, 0)
    step_float = step_index.astype(jnp.float32)
    time_now = 1.0 - (step_float + 1.0) / (STEPS + 2.0)
    time_next = 1.0 - (step_float + 2.0) / (STEPS + 2.0)
    sigma = noise_level * jnp.sqrt(time_now / (1.0 - time_now))
    token_index = (
        lax.axis_index(SEQ) * image_tokens + jnp.arange(image_tokens, dtype=jnp.int32)[None, :]
    )
    channel_index = jnp.arange(latent_now.shape[0], dtype=jnp.int32)[:, None]
    noise = hashed_noise(noise_seeds[0], token_index, channel_index)
    pull = sigma * sigma / (2.0 * time_now)
    span = time_next - time_now
    base = latent_now + pull * latent_now * span + sigma * jnp.sqrt(time_now - time_next) * noise
    slope = (span * (1.0 + pull * (1.0 - time_now))).reshape(1)

    branch = project(heads, weight)
    branch = branch.reshape(4, image_tokens, branch.shape[1])
    branch = lax.all_to_all(branch, "y", split_axis=0, concat_axis=0, tiled=True)
    velocity, stepped = finish(
        slope, branch, image_stream[0], gate, final_weight.transpose(1, 0), base
    )
    velocity = velocity.transpose(1, 0)
    stepped = stepped.transpose(1, 0)
    return (velocity[None], stepped[None], new_master, new_first, new_second, new_average)


def solution(mesh):
    fine = jax.sharding.Mesh(mesh.devices.reshape(16, 2, 2, 4, 2), AXES)
    in_specs = (
        P(DP, SEQ, None, None),
        P(DP, SEQ, None, None),
        P(DP, SEQ, None),
        P(DP, SEQ, None),
        P(DP),
        P(DP),
        P(DP),
        P(),
        P(),
        P(),
        P(DP, None),
        P(DP, SEQ),
        P(DP, SEQ),
        P(DP, SEQ),
        P(DP, SEQ),
        P(DP, SEQ),
    )
    out_specs = (
        P(DP, SEQ, None),
        P(DP, SEQ, None),
        P(DP, SEQ),
        P(DP, SEQ),
        P(DP, SEQ),
        P(DP, SEQ),
    )
    return jax.shard_map(local, mesh=fine, in_specs=in_specs, out_specs=out_specs, check_vma=False)
```

```python
import functools
import math

import jax
import jax.numpy as jnp
from jax import lax
from jax.experimental import pallas as pl
from jax.experimental.pallas import tpu as pltpu
from jax.sharding import PartitionSpec as P

HEAD_DIM = 128
STEPS = 10
STEP_COUNT = 100


beta_first = 0.9
beta_second = 0.999
adam_epsilon = 1e-08
learn_rate = 0.0001
average_decay = 0.99
noise_level = 0.7
norm_epsilon = 1e-06


def hashed_noise(seed_value, token_index, channel_index):
    mixed_bits = seed_value * 73856093 + token_index * 19349663 + channel_index * 83492791
    mixed_bits = mixed_bits ^ jnp.right_shift(mixed_bits, 13)
    mixed_bits = mixed_bits * 1274126177
    mixed_bits = mixed_bits ^ jnp.right_shift(mixed_bits, 16)
    low_bits = mixed_bits & 65535
    return ((low_bits.astype(jnp.float32) + 0.5) / 32768.0 - 1.0) * math.sqrt(3.0)


AXES = ("z", "xl", "xh", "y", "c")
DP = ("z", "xl")
SEQ = ("xh", "y", "c")
MEBI = 1024 * 1024
VMEM = pl.BlockSpec(memory_space=pltpu.VMEM)
SMEM = pl.BlockSpec(memory_space=pltpu.SMEM)


def pack_kernel(image_ref, text_ref, out_ref):
    heads, _, _, width = out_ref.shape
    image_tokens = image_ref.shape[1]
    for head in range(heads):
        span = slice(head * width, (head + 1) * width)
        out_ref[head, :, :image_tokens, :] = image_ref[:, :, span]
        out_ref[head, :, image_tokens:, :] = text_ref[:, :, span]


def pack(image, text):
    tokens = image.shape[1] + text.shape[1]
    return pl.pallas_call(
        pack_kernel,
        out_shape=jax.ShapeDtypeStruct((16, 3, tokens, HEAD_DIM), jnp.bfloat16),
        in_specs=[VMEM, VMEM],
        out_specs=VMEM,
        compiler_params=pltpu.CompilerParams(vmem_limit_bytes=16 * MEBI),
        name="pack",
    )(image, text)


def attention_kernel(packed_ref, out_ref, widened_ref, scores_ref):
    sources, _, tokens, width = packed_ref.shape
    image_tokens = out_ref.shape[2]
    scale = width ** (-0.5) * math.log2(math.e)
    keys = packed_ref[:, 1].reshape(sources * tokens, width)
    widened_ref[:, :width] = packed_ref[:, 2].reshape(sources * tokens, width)
    widened_ref[:, width:] = jnp.ones((sources * tokens, width), jnp.bfloat16)

    def score(index):
        queries = packed_ref[2 * index : 2 * index + 2, 0, :image_tokens, :]
        scores_ref[index % 2] = lax.dot_general(
            queries.reshape(2 * image_tokens, width),
            keys,
            (((1,), (1,)), ((), ())),
            preferred_element_type=jnp.float32,
        )

    steps = sources // 2
    score(0)
    for index in range(steps):
        if index < steps - 1:
            score(index + 1)
        scores = scores_ref[index % 2]
        peak = jnp.max(scores, axis=-1, keepdims=True)
        expo = jnp.exp2((scores - peak) * scale)
        mixed = jnp.dot(
            expo.astype(jnp.bfloat16), widened_ref[...], preferred_element_type=jnp.float32
        )
        result = (mixed[:, :width] / mixed[:, width:]).astype(jnp.bfloat16)
        half, row = divmod(index, 4)
        for core in range(2):
            block = result[core * image_tokens : (core + 1) * image_tokens]
            for target in range(4):
                out_ref[half * 8 + target * 2 + core, row] = block


def attend(packed, image_tokens):
    sources, _, tokens, width = packed.shape
    return pl.pallas_call(
        attention_kernel,
        out_shape=jax.ShapeDtypeStruct((16, 4, image_tokens, HEAD_DIM), jnp.bfloat16),
        in_specs=[VMEM],
        out_specs=VMEM,
        scratch_shapes=[
            pltpu.VMEM((sources * tokens, 2 * width), jnp.bfloat16),
            pltpu.VMEM((2, 2 * image_tokens, sources * tokens), jnp.float32),
        ],
        compiler_params=pltpu.CompilerParams(vmem_limit_bytes=28 * MEBI),
        cost_estimate=pl.CostEstimate(
            flops=3000000000, bytes_accessed=4000000, transcendentals=5300000
        ),
        name="attend",
    )(packed)


def project_kernel(heads_ref, weight_ref, out_ref, flat_ref, weight_vmem, sems):
    head_count, _, width = heads_ref.shape
    parts = sems.shape[0]
    rows = weight_ref.shape[0] // parts
    copies = []
    for part in range(parts):
        span = pl.ds(part * rows, rows)
        copies.append(
            pltpu.make_async_copy(weight_ref.at[span], weight_vmem.at[span], sems.at[part])
        )
        copies[part].start()
    for head in range(head_count):
        flat_ref[:, head * width : (head + 1) * width] = heads_ref[head]
    total = None
    for part in range(parts):
        copies[part].wait()
        span = slice(part * rows, (part + 1) * rows)
        term = jnp.dot(flat_ref[:, span], weight_vmem[span], preferred_element_type=jnp.float32)
        total = term if total is None else total + term
    out_ref[...] = total.astype(jnp.bfloat16)


def project(heads, weight):
    head_count, tokens, width = heads.shape
    return pl.pallas_call(
        project_kernel,
        out_shape=jax.ShapeDtypeStruct((tokens, weight.shape[1]), jnp.bfloat16),
        in_specs=[VMEM, pl.BlockSpec(memory_space=pltpu.HBM)],
        out_specs=VMEM,
        scratch_shapes=[
            pltpu.VMEM((tokens, head_count * width), jnp.bfloat16),
            pltpu.VMEM(weight.shape, jnp.bfloat16),
            pltpu.SemaphoreType.DMA((4,)),
        ],
        compiler_params=pltpu.CompilerParams(vmem_limit_bytes=24 * MEBI),
        cost_estimate=pl.CostEstimate(
            flops=1600000000, bytes_accessed=6000000, transcendentals=0
        ),
        name="project",
    )(heads, pltpu.with_memory_space_constraint(weight, pltpu.HBM))


def finish_kernel(
    slope_ref, branch_ref, stream_ref, gate_ref, final_ref, base_ref, velocity_ref, stepped_ref, hidden_ref
):
    quarters, _, columns = branch_ref.shape
    half = columns // 2
    features = stream_ref.shape[1]
    total = 0.0
    for far in range(2):
        for quarter in range(quarters):
            start = far * quarters * half + quarter * half
            span = slice(start, start + half)
            part = branch_ref[quarter, :, far * half : (far + 1) * half].astype(jnp.float32)
            hidden = stream_ref[:, span].astype(jnp.float32) + gate_ref[:, span] * part
            hidden_ref[:, span] = hidden
            total = total + jnp.sum(hidden, axis=-1, keepdims=True)
    centered = hidden_ref[...] - total / features
    variance = jnp.sum(centered * centered, axis=-1, keepdims=True) / features
    normalized = (centered * lax.rsqrt(variance + norm_epsilon)).astype(jnp.bfloat16)
    velocity = lax.dot_general(
        final_ref[...],
        normalized,
        (((1,), (1,)), ((), ())),
        preferred_element_type=jnp.float32,
    )
    velocity_ref[...] = velocity
    stepped_ref[...] = base_ref[...] + slope_ref[0] * velocity


def finish(slope, branch, stream, gate, final, base):
    shape = jax.ShapeDtypeStruct(base.shape, jnp.float32)
    return pl.pallas_call(
        finish_kernel,
        out_shape=(shape, shape),
        in_specs=[SMEM, VMEM, VMEM, VMEM, VMEM, VMEM],
        out_specs=(VMEM, VMEM),
        scratch_shapes=[pltpu.VMEM(stream.shape, jnp.float32)],
        compiler_params=pltpu.CompilerParams(vmem_limit_bytes=16 * MEBI),
        name="finish",
    )(slope, branch, stream, gate, final, base)


def deal(bit, blocks, run, keep_ref, give_ref):
    pairs = blocks.reshape((blocks.shape[0] // (2 * run), 2, run) + blocks.shape[1:])
    even = pairs[:, 0].reshape(keep_ref.shape)
    odd = pairs[:, 1].reshape(keep_ref.shape)
    keep_ref[...] = jnp.where(bit == 0, even, odd)
    give_ref[...] = jnp.where(bit == 0, odd, even)


def partial_kernel(run, bit_ref, saved_ref, cotangent_ref, keep_ref, give_ref):
    partial = lax.dot_general(
        saved_ref[...],
        cotangent_ref[...],
        (((0,), (1,)), ((), ())),
        preferred_element_type=jnp.float32,
    ).astype(jnp.bfloat16)
    rows, columns = keep_ref.shape[1:]
    blocks = partial.reshape(partial.shape[0] // rows, rows, columns)
    deal(bit_ref[0], blocks, run, keep_ref, give_ref)


def merge_kernel(run, bit_ref, kept_ref, taken_ref, keep_ref, give_ref):
    total = kept_ref[...].astype(jnp.float32) + taken_ref[...].astype(jnp.float32)
    deal(bit_ref[0], total.astype(jnp.bfloat16), run, keep_ref, give_ref)


def split_call(kernel, run, bit, first, second, blocks, rows, columns, name):
    half = jax.ShapeDtypeStruct((blocks // 2, rows, columns), jnp.bfloat16)
    return pl.pallas_call(
        functools.partial(kernel, run),
        out_shape=(half, half),
        in_specs=[SMEM, VMEM, VMEM],
        out_specs=(VMEM, VMEM),
        compiler_params=pltpu.CompilerParams(vmem_limit_bytes=16 * MEBI),
        name=name,
    )(bit, first, second)


def axis_bit(axis, distance):
    return ((lax.axis_index(axis) // distance) % 2).astype(jnp.int32).reshape(1)


def exchange(value, axis, distance):
    size = lax.axis_size(axis)
    return lax.ppermute(value, axis, [(k, k ^ distance) for k in range(size)])


def beside(own, other, axis, dimension):
    first = lax.axis_index(axis) == 0
    return jnp.concatenate([jnp.where(first, own, other), jnp.where(first, other, own)], dimension)


def local(
    image_projected,
    text_projected,
    image_stream,
    latents,
    timesteps,
    prompts,
    noise_seeds,
    time_gate,
    prompt_gate,
    final_weight,
    saved_attention,
    output_cotangent,
    master_weight,
    first_moment,
    second_moment,
    average_weight,
):
    image_tokens = image_projected.shape[1]
    own_rows, own_columns = master_weight.shape

    packed = pack(image_projected[0].transpose(1, 0, 2), text_projected[0].transpose(1, 0, 2))

    def share(kernel, step, first, second):
        axis, distance, run = order[step]
        return split_call(
            kernel,
            run,
            axis_bit(axis, distance),
            first,
            second,
            32 >> step,
            own_rows,
            own_columns,
            kernel.__name__[:-7],
        )

    order = (("z", 1, 2), ("z", 2, 2), ("xl", 1, 1), ("z", 4, 1), ("z", 8, 1))
    keep, give = share(partial_kernel, 0, saved_attention, output_cotangent.transpose(1, 0))
    taken = exchange(give, "z", 1)

    sampler_weight, keep = lax.optimization_barrier((average_weight.astype(jnp.bfloat16), keep))
    pieces = lax.all_gather(sampler_weight, ("xl", "xh", "c"))
    pieces = pieces.reshape(2, 4, own_rows, own_columns).transpose(0, 2, 1, 3)
    pieces = pieces.reshape(2 * own_rows, 4 * own_columns)
    pieces, taken = lax.optimization_barrier((pieces, taken))
    weight = lax.all_gather(pieces, "z", axis=0, tiled=True)
    arrived = lax.all_to_all(packed, SEQ, split_axis=0, concat_axis=0, tiled=True)

    for step in range(1, len(order)):
        keep, give = share(merge_kernel, step, keep, taken)
        if step == 3:
            keep, give, arrived = lax.optimization_barrier((keep, give, arrived))
        taken = exchange(give, *order[step][:2])

    heads_out = attend(arrived, image_tokens)
    heads = lax.all_to_all(heads_out, SEQ, split_axis=0, concat_axis=0, tiled=True)
    heads, keep, taken = lax.optimization_barrier((heads, keep, taken))
    heads = heads.reshape(16, 4 * image_tokens, HEAD_DIM)

    gradient = keep[0].astype(jnp.float32) + taken[0].astype(jnp.float32)
    new_first = beta_first * first_moment + (1.0 - beta_first) * gradient
    new_second = beta_second * second_moment + (1.0 - beta_second) * gradient * gradient
    first_corr = 1.0 - beta_first**STEP_COUNT
    second_corr = 1.0 - beta_second**STEP_COUNT
    new_master = master_weight - learn_rate * (new_first / first_corr) / (
        jnp.sqrt(new_second / second_corr) + adam_epsilon
    )
    new_average = average_decay * average_weight + (1.0 - average_decay) * new_master

    step_index = timesteps[0]
    prompt_index = prompts[0]
    step_table = jnp.arange(time_gate.shape[0], dtype=jnp.int32)[:, None]
    prompt_table = jnp.arange(prompt_gate.shape[0], dtype=jnp.int32)[:, None]
    gate = jnp.sum(
        jnp.where(step_table == step_index, time_gate.astype(jnp.float32), 0.0), 0, keepdims=True
    )
    gate = gate + jnp.sum(
        jnp.where(prompt_table == prompt_index, prompt_gate.astype(jnp.float32), 0.0),
        0,
        keepdims=True,
    )
    latent_now = latents[0].transpose(1, 0)
    step_float = step_index.astype(jnp.float32)
    time_now = 1.0 - (step_float + 1.0) / (STEPS + 2.0)
    time_next = 1.0 - (step_float + 2.0) / (STEPS + 2.0)
    sigma = noise_level * jnp.sqrt(time_now / (1.0 - time_now))
    token_index = (
        lax.axis_index(SEQ) * image_tokens + jnp.arange(image_tokens, dtype=jnp.int32)[None, :]
    )
    channel_index = jnp.arange(latent_now.shape[0], dtype=jnp.int32)[:, None]
    noise = hashed_noise(noise_seeds[0], token_index, channel_index)
    pull = sigma * sigma / (2.0 * time_now)
    span = time_next - time_now
    base = latent_now + pull * latent_now * span + sigma * jnp.sqrt(time_now - time_next) * noise
    slope = (span * (1.0 + pull * (1.0 - time_now))).reshape(1)

    branch = project(heads, weight)
    branch = branch.reshape(4, image_tokens, branch.shape[1])
    branch = lax.all_to_all(branch, "y", split_axis=0, concat_axis=0, tiled=True)
    velocity, stepped = finish(
        slope, branch, image_stream[0], gate, final_weight.transpose(1, 0), base
    )
    velocity = velocity.transpose(1, 0)
    stepped = stepped.transpose(1, 0)
    return (velocity[None], stepped[None], new_master, new_first, new_second, new_average)


def solution(mesh):
    fine = jax.sharding.Mesh(mesh.devices.reshape(16, 2, 2, 4, 2), AXES)
    in_specs = (
        P(DP, SEQ, None, None),
        P(DP, SEQ, None, None),
        P(DP, SEQ, None),
        P(DP, SEQ, None),
        P(DP),
        P(DP),
        P(DP),
        P(),
        P(),
        P(),
        P(DP, None),
        P(DP, SEQ),
        P(DP, SEQ),
        P(DP, SEQ),
        P(DP, SEQ),
        P(DP, SEQ),
    )
    out_specs = (
        P(DP, SEQ, None),
        P(DP, SEQ, None),
        P(DP, SEQ),
        P(DP, SEQ),
        P(DP, SEQ),
        P(DP, SEQ),
    )
    return jax.shard_map(local, mesh=fine, in_specs=in_specs, out_specs=out_specs, check_vma=False)
```

```python
import functools
import math

import jax
import jax.numpy as jnp
from jax import lax
from jax.experimental import pallas as pl
from jax.experimental.pallas import tpu as pltpu
from jax.sharding import PartitionSpec as P

HEAD_DIM = 128
STEPS = 10
STEP_COUNT = 100


beta_first = 0.9
beta_second = 0.999
adam_epsilon = 1e-08
learn_rate = 0.0001
average_decay = 0.99
noise_level = 0.7
norm_epsilon = 1e-06


def hashed_noise(seed_value, token_index, channel_index):
    mixed_bits = seed_value * 73856093 + token_index * 19349663 + channel_index * 83492791
    mixed_bits = mixed_bits ^ jnp.right_shift(mixed_bits, 13)
    mixed_bits = mixed_bits * 1274126177
    mixed_bits = mixed_bits ^ jnp.right_shift(mixed_bits, 16)
    low_bits = mixed_bits & 65535
    return ((low_bits.astype(jnp.float32) + 0.5) / 32768.0 - 1.0) * math.sqrt(3.0)


AXES = ("z", "xl", "xh", "y", "c")
DP = ("z", "xl")
SEQ = ("xh", "y", "c")
MEBI = 1024 * 1024
VMEM = pl.BlockSpec(memory_space=pltpu.VMEM)
SMEM = pl.BlockSpec(memory_space=pltpu.SMEM)


def pack_kernel(image_ref, text_ref, out_ref):
    heads, _, _, width = out_ref.shape
    image_tokens = image_ref.shape[1]
    for head in range(heads):
        span = slice(head * width, (head + 1) * width)
        out_ref[head, :, :image_tokens, :] = image_ref[:, :, span]
        out_ref[head, :, image_tokens:, :] = text_ref[:, :, span]


def pack(image, text):
    tokens = image.shape[1] + text.shape[1]
    return pl.pallas_call(
        pack_kernel,
        out_shape=jax.ShapeDtypeStruct((16, 3, tokens, HEAD_DIM), jnp.bfloat16),
        in_specs=[VMEM, VMEM],
        out_specs=VMEM,
        compiler_params=pltpu.CompilerParams(vmem_limit_bytes=16 * MEBI),
        name="pack",
    )(image, text)


def attention_kernel(packed_ref, out_ref, widened_ref, scores_ref):
    sources, _, tokens, width = packed_ref.shape
    image_tokens = out_ref.shape[2]
    scale = width ** (-0.5) * math.log2(math.e)
    keys = packed_ref[:, 1].reshape(sources * tokens, width)
    widened_ref[:, :width] = packed_ref[:, 2].reshape(sources * tokens, width)
    widened_ref[:, width:] = jnp.ones((sources * tokens, width), jnp.bfloat16)

    def score(index):
        queries = packed_ref[2 * index : 2 * index + 2, 0, :image_tokens, :]
        scores_ref[index % 2] = lax.dot_general(
            queries.reshape(2 * image_tokens, width),
            keys,
            (((1,), (1,)), ((), ())),
            preferred_element_type=jnp.float32,
        )

    steps = sources // 2
    score(0)
    for index in range(steps):
        if index < steps - 1:
            score(index + 1)
        scores = scores_ref[index % 2]
        peak = jnp.max(scores, axis=-1, keepdims=True)
        expo = jnp.exp2((scores - peak) * scale)
        mixed = jnp.dot(
            expo.astype(jnp.bfloat16), widened_ref[...], preferred_element_type=jnp.float32
        )
        result = (mixed[:, :width] / mixed[:, width:]).astype(jnp.bfloat16)
        half, row = divmod(index, 4)
        for core in range(2):
            block = result[core * image_tokens : (core + 1) * image_tokens]
            for target in range(4):
                out_ref[half * 8 + target * 2 + core, row] = block


def attend(packed, image_tokens):
    sources, _, tokens, width = packed.shape
    return pl.pallas_call(
        attention_kernel,
        out_shape=jax.ShapeDtypeStruct((16, 4, image_tokens, HEAD_DIM), jnp.bfloat16),
        in_specs=[VMEM],
        out_specs=VMEM,
        scratch_shapes=[
            pltpu.VMEM((sources * tokens, 2 * width), jnp.bfloat16),
            pltpu.VMEM((2, 2 * image_tokens, sources * tokens), jnp.float32),
        ],
        compiler_params=pltpu.CompilerParams(vmem_limit_bytes=28 * MEBI),
        cost_estimate=pl.CostEstimate(
            flops=3000000000, bytes_accessed=4000000, transcendentals=5300000
        ),
        name="attend",
    )(packed)


def project_kernel(heads_ref, weight_ref, out_ref, flat_ref, weight_vmem, sems):
    head_count, _, width = heads_ref.shape
    parts = sems.shape[0]
    rows = weight_ref.shape[0] // parts
    copies = []
    for part in range(parts):
        span = pl.ds(part * rows, rows)
        copies.append(
            pltpu.make_async_copy(weight_ref.at[span], weight_vmem.at[span], sems.at[part])
        )
        copies[part].start()
    for head in range(head_count):
        flat_ref[:, head * width : (head + 1) * width] = heads_ref[head]
    total = None
    for part in range(parts):
        copies[part].wait()
        span = slice(part * rows, (part + 1) * rows)
        term = jnp.dot(flat_ref[:, span], weight_vmem[span], preferred_element_type=jnp.float32)
        total = term if total is None else total + term
    out_ref[...] = total.astype(jnp.bfloat16)


def project(heads, weight):
    head_count, tokens, width = heads.shape
    return pl.pallas_call(
        project_kernel,
        out_shape=jax.ShapeDtypeStruct((tokens, weight.shape[1]), jnp.bfloat16),
        in_specs=[VMEM, pl.BlockSpec(memory_space=pltpu.HBM)],
        out_specs=VMEM,
        scratch_shapes=[
            pltpu.VMEM((tokens, head_count * width), jnp.bfloat16),
            pltpu.VMEM(weight.shape, jnp.bfloat16),
            pltpu.SemaphoreType.DMA((4,)),
        ],
        compiler_params=pltpu.CompilerParams(vmem_limit_bytes=24 * MEBI),
        cost_estimate=pl.CostEstimate(
            flops=1600000000, bytes_accessed=6000000, transcendentals=0
        ),
        name="project",
    )(heads, pltpu.with_memory_space_constraint(weight, pltpu.HBM))


def finish_kernel(
    slope_ref, branch_ref, stream_ref, gate_ref, final_ref, base_ref, velocity_ref, stepped_ref, hidden_ref
):
    quarters, _, columns = branch_ref.shape
    half = columns // 2
    features = stream_ref.shape[1]
    total = 0.0
    for far in range(2):
        for quarter in range(quarters):
            start = far * quarters * half + quarter * half
            span = slice(start, start + half)
            part = branch_ref[quarter, :, far * half : (far + 1) * half].astype(jnp.float32)
            hidden = stream_ref[:, span].astype(jnp.float32) + gate_ref[:, span] * part
            hidden_ref[:, span] = hidden
            total = total + jnp.sum(hidden, axis=-1, keepdims=True)
    centered = hidden_ref[...] - total / features
    variance = jnp.sum(centered * centered, axis=-1, keepdims=True) / features
    normalized = (centered * lax.rsqrt(variance + norm_epsilon)).astype(jnp.bfloat16)
    velocity = lax.dot_general(
        final_ref[...],
        normalized,
        (((1,), (1,)), ((), ())),
        preferred_element_type=jnp.float32,
    )
    velocity_ref[...] = velocity
    stepped_ref[...] = base_ref[...] + slope_ref[0] * velocity


def finish(slope, branch, stream, gate, final, base):
    shape = jax.ShapeDtypeStruct(base.shape, jnp.float32)
    return pl.pallas_call(
        finish_kernel,
        out_shape=(shape, shape),
        in_specs=[SMEM, VMEM, VMEM, VMEM, VMEM, VMEM],
        out_specs=(VMEM, VMEM),
        scratch_shapes=[pltpu.VMEM(stream.shape, jnp.float32)],
        compiler_params=pltpu.CompilerParams(vmem_limit_bytes=16 * MEBI),
        name="finish",
    )(slope, branch, stream, gate, final, base)


def deal(bit, blocks, run, keep_ref, give_ref):
    pairs = blocks.reshape((blocks.shape[0] // (2 * run), 2, run) + blocks.shape[1:])
    even = pairs[:, 0].reshape(keep_ref.shape)
    odd = pairs[:, 1].reshape(keep_ref.shape)
    keep_ref[...] = jnp.where(bit == 0, even, odd)
    give_ref[...] = jnp.where(bit == 0, odd, even)


def partial_kernel(run, bit_ref, saved_ref, cotangent_ref, keep_ref, give_ref):
    partial = lax.dot_general(
        saved_ref[...],
        cotangent_ref[...],
        (((0,), (1,)), ((), ())),
        preferred_element_type=jnp.float32,
    ).astype(jnp.bfloat16)
    rows, columns = keep_ref.shape[1:]
    blocks = partial.reshape(partial.shape[0] // rows, rows, columns)
    deal(bit_ref[0], blocks, run, keep_ref, give_ref)


def merge_kernel(run, bit_ref, kept_ref, taken_ref, keep_ref, give_ref):
    total = kept_ref[...].astype(jnp.float32) + taken_ref[...].astype(jnp.float32)
    deal(bit_ref[0], total.astype(jnp.bfloat16), run, keep_ref, give_ref)


def split_call(kernel, run, bit, first, second, blocks, rows, columns, name):
    half = jax.ShapeDtypeStruct((blocks // 2, rows, columns), jnp.bfloat16)
    return pl.pallas_call(
        functools.partial(kernel, run),
        out_shape=(half, half),
        in_specs=[SMEM, VMEM, VMEM],
        out_specs=(VMEM, VMEM),
        compiler_params=pltpu.CompilerParams(vmem_limit_bytes=16 * MEBI),
        name=name,
    )(bit, first, second)


def axis_bit(axis, distance):
    return ((lax.axis_index(axis) // distance) % 2).astype(jnp.int32).reshape(1)


def exchange(value, axis, distance):
    size = lax.axis_size(axis)
    return lax.ppermute(value, axis, [(k, k ^ distance) for k in range(size)])


def beside(own, other, axis, dimension):
    first = lax.axis_index(axis) == 0
    return jnp.concatenate([jnp.where(first, own, other), jnp.where(first, other, own)], dimension)


def local(
    image_projected,
    text_projected,
    image_stream,
    latents,
    timesteps,
    prompts,
    noise_seeds,
    time_gate,
    prompt_gate,
    final_weight,
    saved_attention,
    output_cotangent,
    master_weight,
    first_moment,
    second_moment,
    average_weight,
):
    image_tokens = image_projected.shape[1]
    own_rows, own_columns = master_weight.shape

    packed = pack(image_projected[0].transpose(1, 0, 2), text_projected[0].transpose(1, 0, 2))

    def share(kernel, step, first, second):
        axis, distance, run = order[step]
        return split_call(
            kernel,
            run,
            axis_bit(axis, distance),
            first,
            second,
            32 >> step,
            own_rows,
            own_columns,
            kernel.__name__[:-7],
        )

    order = (("z", 1, 2), ("z", 2, 2), ("xl", 1, 1), ("z", 4, 1), ("z", 8, 1))
    keep, give = share(partial_kernel, 0, saved_attention, output_cotangent.transpose(1, 0))
    taken = exchange(give, "z", 1)

    sampler_weight, keep = lax.optimization_barrier((average_weight.astype(jnp.bfloat16), keep))
    gathered = lax.all_gather(sampler_weight, ("xl", "xh", "c"))
    pieces = jnp.concatenate(
        [jnp.concatenate([gathered[4 * half + k] for k in range(4)], 1) for half in range(2)], 0
    )
    pieces, taken = lax.optimization_barrier((pieces, taken))
    weight = lax.all_gather(pieces, "z", axis=0, tiled=True)
    arrived = lax.all_to_all(packed, SEQ, split_axis=0, concat_axis=0, tiled=True)

    for step in range(1, len(order)):
        keep, give = share(merge_kernel, step, keep, taken)
        if step == 3:
            keep, give, arrived = lax.optimization_barrier((keep, give, arrived))
        taken = exchange(give, *order[step][:2])

    heads_out = attend(arrived, image_tokens)
    heads = lax.all_to_all(heads_out, SEQ, split_axis=0, concat_axis=0, tiled=True)
    heads, keep, taken = lax.optimization_barrier((heads, keep, taken))
    heads = heads.reshape(16, 4 * image_tokens, HEAD_DIM)

    gradient = keep[0].astype(jnp.float32) + taken[0].astype(jnp.float32)
    new_first = beta_first * first_moment + (1.0 - beta_first) * gradient
    new_second = beta_second * second_moment + (1.0 - beta_second) * gradient * gradient
    first_corr = 1.0 - beta_first**STEP_COUNT
    second_corr = 1.0 - beta_second**STEP_COUNT
    new_master = master_weight - learn_rate * (new_first / first_corr) / (
        jnp.sqrt(new_second / second_corr) + adam_epsilon
    )
    new_average = average_decay * average_weight + (1.0 - average_decay) * new_master

    step_index = timesteps[0]
    prompt_index = prompts[0]
    step_table = jnp.arange(time_gate.shape[0], dtype=jnp.int32)[:, None]
    prompt_table = jnp.arange(prompt_gate.shape[0], dtype=jnp.int32)[:, None]
    gate = jnp.sum(
        jnp.where(step_table == step_index, time_gate.astype(jnp.float32), 0.0), 0, keepdims=True
    )
    gate = gate + jnp.sum(
        jnp.where(prompt_table == prompt_index, prompt_gate.astype(jnp.float32), 0.0),
        0,
        keepdims=True,
    )
    latent_now = latents[0].transpose(1, 0)
    step_float = step_index.astype(jnp.float32)
    time_now = 1.0 - (step_float + 1.0) / (STEPS + 2.0)
    time_next = 1.0 - (step_float + 2.0) / (STEPS + 2.0)
    sigma = noise_level * jnp.sqrt(time_now / (1.0 - time_now))
    token_index = (
        lax.axis_index(SEQ) * image_tokens + jnp.arange(image_tokens, dtype=jnp.int32)[None, :]
    )
    channel_index = jnp.arange(latent_now.shape[0], dtype=jnp.int32)[:, None]
    noise = hashed_noise(noise_seeds[0], token_index, channel_index)
    pull = sigma * sigma / (2.0 * time_now)
    span = time_next - time_now
    base = latent_now + pull * latent_now * span + sigma * jnp.sqrt(time_now - time_next) * noise
    slope = (span * (1.0 + pull * (1.0 - time_now))).reshape(1)

    branch = project(heads, weight)
    branch = branch.reshape(4, image_tokens, branch.shape[1])
    branch = lax.all_to_all(branch, "y", split_axis=0, concat_axis=0, tiled=True)
    velocity, stepped = finish(
        slope, branch, image_stream[0], gate, final_weight.transpose(1, 0), base
    )
    velocity = velocity.transpose(1, 0)
    stepped = stepped.transpose(1, 0)
    return (velocity[None], stepped[None], new_master, new_first, new_second, new_average)


def solution(mesh):
    fine = jax.sharding.Mesh(mesh.devices.reshape(16, 2, 2, 4, 2), AXES)
    in_specs = (
        P(DP, SEQ, None, None),
        P(DP, SEQ, None, None),
        P(DP, SEQ, None),
        P(DP, SEQ, None),
        P(DP),
        P(DP),
        P(DP),
        P(),
        P(),
        P(),
        P(DP, None),
        P(DP, SEQ),
        P(DP, SEQ),
        P(DP, SEQ),
        P(DP, SEQ),
        P(DP, SEQ),
    )
    out_specs = (
        P(DP, SEQ, None),
        P(DP, SEQ, None),
        P(DP, SEQ),
        P(DP, SEQ),
        P(DP, SEQ),
        P(DP, SEQ),
    )
    return jax.shard_map(local, mesh=fine, in_specs=in_specs, out_specs=out_specs, check_vma=False)
```

```python
import functools
import math

import jax
import jax.numpy as jnp
from jax import lax
from jax.experimental import pallas as pl
from jax.experimental.pallas import tpu as pltpu
from jax.sharding import PartitionSpec as P

HEAD_DIM = 128
STEPS = 10
STEP_COUNT = 100


beta_first = 0.9
beta_second = 0.999
adam_epsilon = 1e-08
learn_rate = 0.0001
average_decay = 0.99
noise_level = 0.7
norm_epsilon = 1e-06


def hashed_noise(seed_value, token_index, channel_index):
    mixed_bits = seed_value * 73856093 + token_index * 19349663 + channel_index * 83492791
    mixed_bits = mixed_bits ^ jnp.right_shift(mixed_bits, 13)
    mixed_bits = mixed_bits * 1274126177
    mixed_bits = mixed_bits ^ jnp.right_shift(mixed_bits, 16)
    low_bits = mixed_bits & 65535
    return ((low_bits.astype(jnp.float32) + 0.5) / 32768.0 - 1.0) * math.sqrt(3.0)


AXES = ("z", "xl", "xh", "y", "c")
DP = ("z", "xl")
SEQ = ("xh", "y", "c")
MEBI = 1024 * 1024
VMEM = pl.BlockSpec(memory_space=pltpu.VMEM)
SMEM = pl.BlockSpec(memory_space=pltpu.SMEM)


def pack_kernel(image_ref, text_ref, out_ref):
    heads, _, _, width = out_ref.shape
    image_tokens = image_ref.shape[1]
    for head in range(heads):
        span = slice(head * width, (head + 1) * width)
        out_ref[head, :, :image_tokens, :] = image_ref[:, :, span]
        out_ref[head, :, image_tokens:, :] = text_ref[:, :, span]


def pack(image, text):
    tokens = image.shape[1] + text.shape[1]
    return pl.pallas_call(
        pack_kernel,
        out_shape=jax.ShapeDtypeStruct((16, 3, tokens, HEAD_DIM), jnp.bfloat16),
        in_specs=[VMEM, VMEM],
        out_specs=VMEM,
        compiler_params=pltpu.CompilerParams(vmem_limit_bytes=16 * MEBI),
        name="pack",
    )(image, text)


def attention_kernel(packed_ref, out_ref, widened_ref, scores_ref):
    sources, _, tokens, width = packed_ref.shape
    image_tokens = out_ref.shape[2]
    scale = width ** (-0.5) * math.log2(math.e)
    keys = packed_ref[:, 1].reshape(sources * tokens, width)
    widened_ref[:, :width] = packed_ref[:, 2].reshape(sources * tokens, width)
    widened_ref[:, width:] = jnp.ones((sources * tokens, width), jnp.bfloat16)

    def score(index):
        queries = packed_ref[2 * index : 2 * index + 2, 0, :image_tokens, :]
        scores_ref[index % 2] = lax.dot_general(
            queries.reshape(2 * image_tokens, width),
            keys,
            (((1,), (1,)), ((), ())),
            preferred_element_type=jnp.float32,
        )

    steps = sources // 2
    score(0)
    for index in range(steps):
        if index < steps - 1:
            score(index + 1)
        scores = scores_ref[index % 2]
        peak = jnp.max(scores, axis=-1, keepdims=True)
        expo = jnp.exp2((scores - peak) * scale)
        mixed = jnp.dot(
            expo.astype(jnp.bfloat16), widened_ref[...], preferred_element_type=jnp.float32
        )
        result = (mixed[:, :width] / mixed[:, width:]).astype(jnp.bfloat16)
        half, row = divmod(index, 4)
        for core in range(2):
            block = result[core * image_tokens : (core + 1) * image_tokens]
            for target in range(4):
                out_ref[half * 8 + target * 2 + core, row] = block


def attend(packed, image_tokens):
    sources, _, tokens, width = packed.shape
    return pl.pallas_call(
        attention_kernel,
        out_shape=jax.ShapeDtypeStruct((16, 4, image_tokens, HEAD_DIM), jnp.bfloat16),
        in_specs=[VMEM],
        out_specs=VMEM,
        scratch_shapes=[
            pltpu.VMEM((sources * tokens, 2 * width), jnp.bfloat16),
            pltpu.VMEM((2, 2 * image_tokens, sources * tokens), jnp.float32),
        ],
        compiler_params=pltpu.CompilerParams(vmem_limit_bytes=28 * MEBI),
        cost_estimate=pl.CostEstimate(
            flops=3000000000, bytes_accessed=4000000, transcendentals=5300000
        ),
        name="attend",
    )(packed)


def project_kernel(heads_ref, weight_ref, out_ref, flat_ref, weight_vmem, sems):
    head_count, _, width = heads_ref.shape
    parts = sems.shape[0]
    rows = weight_ref.shape[0] // parts
    copies = []
    for part in range(parts):
        span = pl.ds(part * rows, rows)
        copies.append(
            pltpu.make_async_copy(weight_ref.at[span], weight_vmem.at[span], sems.at[part])
        )
        copies[part].start()
    for head in range(head_count):
        flat_ref[:, head * width : (head + 1) * width] = heads_ref[head]
    total = None
    for part in range(parts):
        copies[part].wait()
        span = slice(part * rows, (part + 1) * rows)
        term = jnp.dot(flat_ref[:, span], weight_vmem[span], preferred_element_type=jnp.float32)
        total = term if total is None else total + term
    out_ref[...] = total.astype(jnp.bfloat16)


def project(heads, weight):
    head_count, tokens, width = heads.shape
    return pl.pallas_call(
        project_kernel,
        out_shape=jax.ShapeDtypeStruct((tokens, weight.shape[1]), jnp.bfloat16),
        in_specs=[VMEM, pl.BlockSpec(memory_space=pltpu.HBM)],
        out_specs=VMEM,
        scratch_shapes=[
            pltpu.VMEM((tokens, head_count * width), jnp.bfloat16),
            pltpu.VMEM(weight.shape, jnp.bfloat16),
            pltpu.SemaphoreType.DMA((2,)),
        ],
        compiler_params=pltpu.CompilerParams(vmem_limit_bytes=24 * MEBI),
        cost_estimate=pl.CostEstimate(
            flops=1600000000, bytes_accessed=6000000, transcendentals=0
        ),
        name="project",
    )(heads, pltpu.with_memory_space_constraint(weight, pltpu.HBM))


def finish_kernel(
    slope_ref, branch_ref, stream_ref, gate_ref, final_ref, base_ref, velocity_ref, stepped_ref, hidden_ref
):
    quarters, _, columns = branch_ref.shape
    half = columns // 2
    features = stream_ref.shape[1]
    total = 0.0
    for far in range(2):
        for quarter in range(quarters):
            start = far * quarters * half + quarter * half
            span = slice(start, start + half)
            part = branch_ref[quarter, :, far * half : (far + 1) * half].astype(jnp.float32)
            hidden = stream_ref[:, span].astype(jnp.float32) + gate_ref[:, span] * part
            hidden_ref[:, span] = hidden
            total = total + jnp.sum(hidden, axis=-1, keepdims=True)
    centered = hidden_ref[...] - total / features
    variance = jnp.sum(centered * centered, axis=-1, keepdims=True) / features
    normalized = (centered * lax.rsqrt(variance + norm_epsilon)).astype(jnp.bfloat16)
    velocity = lax.dot_general(
        final_ref[...],
        normalized,
        (((1,), (1,)), ((), ())),
        preferred_element_type=jnp.float32,
    )
    velocity_ref[...] = velocity
    stepped_ref[...] = base_ref[...] + slope_ref[0] * velocity


def finish(slope, branch, stream, gate, final, base):
    shape = jax.ShapeDtypeStruct(base.shape, jnp.float32)
    return pl.pallas_call(
        finish_kernel,
        out_shape=(shape, shape),
        in_specs=[SMEM, VMEM, VMEM, VMEM, VMEM, VMEM],
        out_specs=(VMEM, VMEM),
        scratch_shapes=[pltpu.VMEM(stream.shape, jnp.float32)],
        compiler_params=pltpu.CompilerParams(vmem_limit_bytes=16 * MEBI),
        name="finish",
    )(slope, branch, stream, gate, final, base)


def deal(bit, blocks, run, keep_ref, give_ref):
    pairs = blocks.reshape((blocks.shape[0] // (2 * run), 2, run) + blocks.shape[1:])
    even = pairs[:, 0].reshape(keep_ref.shape)
    odd = pairs[:, 1].reshape(keep_ref.shape)
    keep_ref[...] = jnp.where(bit == 0, even, odd)
    give_ref[...] = jnp.where(bit == 0, odd, even)


def partial_kernel(run, bit_ref, saved_ref, cotangent_ref, keep_ref, give_ref):
    partial = lax.dot_general(
        saved_ref[...],
        cotangent_ref[...],
        (((0,), (1,)), ((), ())),
        preferred_element_type=jnp.float32,
    ).astype(jnp.bfloat16)
    rows, columns = keep_ref.shape[1:]
    blocks = partial.reshape(partial.shape[0] // rows, rows, columns)
    deal(bit_ref[0], blocks, run, keep_ref, give_ref)


def merge_kernel(run, bit_ref, kept_ref, taken_ref, keep_ref, give_ref):
    total = kept_ref[...].astype(jnp.float32) + taken_ref[...].astype(jnp.float32)
    deal(bit_ref[0], total.astype(jnp.bfloat16), run, keep_ref, give_ref)


def split_call(kernel, run, bit, first, second, blocks, rows, columns, name):
    half = jax.ShapeDtypeStruct((blocks // 2, rows, columns), jnp.bfloat16)
    return pl.pallas_call(
        functools.partial(kernel, run),
        out_shape=(half, half),
        in_specs=[SMEM, VMEM, VMEM],
        out_specs=(VMEM, VMEM),
        compiler_params=pltpu.CompilerParams(vmem_limit_bytes=16 * MEBI),
        name=name,
    )(bit, first, second)


def axis_bit(axis, distance):
    return ((lax.axis_index(axis) // distance) % 2).astype(jnp.int32).reshape(1)


def exchange(value, axis, distance):
    size = lax.axis_size(axis)
    return lax.ppermute(value, axis, [(k, k ^ distance) for k in range(size)])


def beside(own, other, axis, dimension):
    first = lax.axis_index(axis) == 0
    return jnp.concatenate([jnp.where(first, own, other), jnp.where(first, other, own)], dimension)


def local(
    image_projected,
    text_projected,
    image_stream,
    latents,
    timesteps,
    prompts,
    noise_seeds,
    time_gate,
    prompt_gate,
    final_weight,
    saved_attention,
    output_cotangent,
    master_weight,
    first_moment,
    second_moment,
    average_weight,
):
    image_tokens = image_projected.shape[1]
    own_rows, own_columns = master_weight.shape

    packed = pack(image_projected[0].transpose(1, 0, 2), text_projected[0].transpose(1, 0, 2))

    def share(kernel, step, first, second, bit=None):
        axis, distance, run = order[step]
        return split_call(
            kernel,
            run,
            axis_bit(axis, distance) if bit is None else bit,
            first,
            second,
            32 >> step,
            own_rows,
            own_columns,
            kernel.__name__[:-7],
        )

    order = (("z", 1, 2), ("z", 2, 2), ("xl", 1, 1), ("z", 4, 1), ("z", 8, 1))
    sampler_weight, first_bit = lax.optimization_barrier(
        (average_weight.astype(jnp.bfloat16), axis_bit("z", 1))
    )
    keep, give = share(
        partial_kernel, 0, saved_attention, output_cotangent.transpose(1, 0), first_bit
    )
    taken = exchange(give, "z", 1)

    sampler_weight, keep = lax.optimization_barrier((sampler_weight, keep))
    gathered = lax.all_gather(sampler_weight, ("xl", "xh", "c"))
    pieces = jnp.concatenate(
        [jnp.concatenate([gathered[4 * half + k] for k in range(4)], 1) for half in range(2)], 0
    )
    pieces, taken = lax.optimization_barrier((pieces, taken))
    weight = lax.all_gather(pieces, "z", axis=0, tiled=True)
    arrived = lax.all_to_all(packed, SEQ, split_axis=0, concat_axis=0, tiled=True)

    for step in range(1, len(order)):
        keep, give = share(merge_kernel, step, keep, taken)
        if step == 3:
            keep, give, arrived = lax.optimization_barrier((keep, give, arrived))
        taken = exchange(give, *order[step][:2])

    heads_out = attend(arrived, image_tokens)
    heads = lax.all_to_all(heads_out, SEQ, split_axis=0, concat_axis=0, tiled=True)
    heads, keep, taken = lax.optimization_barrier((heads, keep, taken))
    heads = heads.reshape(16, 4 * image_tokens, HEAD_DIM)

    gradient = keep[0].astype(jnp.float32) + taken[0].astype(jnp.float32)
    new_first = beta_first * first_moment + (1.0 - beta_first) * gradient
    new_second = beta_second * second_moment + (1.0 - beta_second) * gradient * gradient
    first_corr = 1.0 - beta_first**STEP_COUNT
    second_corr = 1.0 - beta_second**STEP_COUNT
    new_master = master_weight - learn_rate * (new_first / first_corr) / (
        jnp.sqrt(new_second / second_corr) + adam_epsilon
    )
    new_average = average_decay * average_weight + (1.0 - average_decay) * new_master

    step_index = timesteps[0]
    prompt_index = prompts[0]
    step_table = jnp.arange(time_gate.shape[0], dtype=jnp.int32)[:, None]
    prompt_table = jnp.arange(prompt_gate.shape[0], dtype=jnp.int32)[:, None]
    gate = jnp.sum(
        jnp.where(step_table == step_index, time_gate.astype(jnp.float32), 0.0), 0, keepdims=True
    )
    gate = gate + jnp.sum(
        jnp.where(prompt_table == prompt_index, prompt_gate.astype(jnp.float32), 0.0),
        0,
        keepdims=True,
    )
    latent_now = latents[0].transpose(1, 0)
    step_float = step_index.astype(jnp.float32)
    time_now = 1.0 - (step_float + 1.0) / (STEPS + 2.0)
    time_next = 1.0 - (step_float + 2.0) / (STEPS + 2.0)
    sigma = noise_level * jnp.sqrt(time_now / (1.0 - time_now))
    token_index = (
        lax.axis_index(SEQ) * image_tokens + jnp.arange(image_tokens, dtype=jnp.int32)[None, :]
    )
    channel_index = jnp.arange(latent_now.shape[0], dtype=jnp.int32)[:, None]
    noise = hashed_noise(noise_seeds[0], token_index, channel_index)
    pull = sigma * sigma / (2.0 * time_now)
    span = time_next - time_now
    base = latent_now + pull * latent_now * span + sigma * jnp.sqrt(time_now - time_next) * noise
    slope = (span * (1.0 + pull * (1.0 - time_now))).reshape(1)

    branch = project(heads, weight)
    branch = branch.reshape(4, image_tokens, branch.shape[1])
    branch = lax.all_to_all(branch, "y", split_axis=0, concat_axis=0, tiled=True)
    velocity, stepped = finish(
        slope, branch, image_stream[0], gate, final_weight.transpose(1, 0), base
    )
    velocity = velocity.transpose(1, 0)
    stepped = stepped.transpose(1, 0)
    return (velocity[None], stepped[None], new_master, new_first, new_second, new_average)


def solution(mesh):
    fine = jax.sharding.Mesh(mesh.devices.reshape(16, 2, 2, 4, 2), AXES)
    in_specs = (
        P(DP, SEQ, None, None),
        P(DP, SEQ, None, None),
        P(DP, SEQ, None),
        P(DP, SEQ, None),
        P(DP),
        P(DP),
        P(DP),
        P(),
        P(),
        P(),
        P(DP, None),
        P(DP, SEQ),
        P(DP, SEQ),
        P(DP, SEQ),
        P(DP, SEQ),
        P(DP, SEQ),
    )
    out_specs = (
        P(DP, SEQ, None),
        P(DP, SEQ, None),
        P(DP, SEQ),
        P(DP, SEQ),
        P(DP, SEQ),
        P(DP, SEQ),
    )
    return jax.shard_map(local, mesh=fine, in_specs=in_specs, out_specs=out_specs, check_vma=False)
```
